32 devices in a mesh: parts: 2 (over y), dp: 4 (over z), layer: 2 (over x), module: 2 (over core).
Axes of the slice: x: 2, y: 2, z: 4, core: 2. Of those that a mesh axis runs over, the one named last changes fastest.
Arguments:
- train_acts: bfloat16 [8, 128, 32, 1024], P(('layer', 'module'), ('parts', 'dp')), parts along dimension 1, may hold values from -6 to 6
- train_grads: bfloat16 [8, 128, 32, 1024], P(('layer', 'module'), ('parts', 'dp')), parts along dimension 1, may hold values from -6 to 6
- lengths: int32 [128], P(('parts', 'dp')), parts along dimension 0, may hold values from 256 to 1024
- query_grads: bfloat16 [1024, 8, 1024], P(('parts', 'dp'), ('layer', 'module')), parts along dimension 0, may hold values from -0.0078125 to 0.0078125
- inv_in: float32 [8, 32, 32], P(('layer', 'module')), may hold values from -1 to 4, as said below
- inv_out: float32 [8, 32, 32], P(('layer', 'module')), may hold values from -1 to 4, as said below
- query_ids: int32 [1024], P('parts'), parts along dimension 0, may hold values from 0 to 63
Outputs:
- influence: float32 [128, 512], P(('parts', 'dp'), ('layer', 'module')), parts along dimension 0
The draws below stay inside these ranges and needn't reach their ends.
There are 2 independent parts, one for each index of `parts`. The reference program is written for one: setup_inputs(seed, part) draws one part's arguments, and reference() takes and returns one part's arrays. A program takes and returns all parts, laid end to end along the dimension named above; an argument that names none is the same for every part. Nothing has to cross between parts.
Inputs may be any that keep to these rules, and one draw needn't show every extreme that they name: `inv_in`: symmetric. `inv_out`: symmetric.
All inputs are finite; a program needn't handle non-finite values.
Results may differ from the reference program's by a relative error of at most 0.0041.
Values may be sent and summed in bfloat16 or wider, within the bound.
A program may use at most 64 MiB of HBM per device.

```python
import math
import jax
import jax.numpy as jnp
from jax import lax

RANK = 32
SEQ = 1024
QUERIES = 512
MODULES = 8
EXAMPLES = 64


def precond_factor(key, low_diag, high_diag):
    key_diag, key_off = jax.random.split(key)
    diagonal = jnp.exp(jax.random.uniform(key_diag, (MODULES, RANK), jnp.float32, math.log(low_diag), math.log(high_diag)))
    jitter = jnp.clip(jax.random.normal(key_off, (MODULES, RANK, RANK), jnp.float32), -3.0, 3.0) * 0.08
    symmetric = (jitter + jnp.swapaxes(jitter, 1, 2)) * 0.5
    identity = jnp.eye(RANK, dtype=jnp.float32)
    return symmetric * (1.0 - identity) + identity * diagonal[:, :, None]


def draw_inv_in(key, part):
    key = jax.random.fold_in(key, 11)
    return precond_factor(key, 0.5, 2.0)


def draw_inv_out(key, part):
    key = jax.random.fold_in(key, 23)
    return precond_factor(key, 0.5, 2.0)


def plant(result, own_key, low, high):
    spot = [jax.random.randint(jax.random.fold_in(own_key, axis), (), 0, length) for axis, length in enumerate(result.shape)]
    widest = result.shape.index(max(result.shape))
    neighbour = spot[:widest] + [(spot[widest] + 1) % result.shape[widest]] + spot[widest + 1:]
    return result.at[tuple(spot)].set(low).at[tuple(neighbour)].set(high)


def block_scale(own_key, shape, pieces, least, largest):
    level, own = 1.0, jax.random.fold_in(own_key, 6)
    for position, parts in pieces:
        draws = jnp.exp(jax.random.uniform(jax.random.fold_in(own, position), (parts,), jnp.float32, least / len(pieces), largest / len(pieces)))
        level = level * jnp.repeat(draws, shape[position] // parts).reshape([-1 if axis == position else 1 for axis in range(len(shape))])
    return level


def normal_values(key, shape, width, limit, pieces=(), kind=jnp.bfloat16):
    values = jax.random.normal(key, shape, jnp.float32) * width
    if len(pieces) > 0:
        values = block_scale(key, shape, pieces, -0.22, 0.18) * values
    return jnp.clip(values, min=-limit, max=limit).astype(kind)


def setup_inputs(seed: int = 0, part: int = 0) -> dict:
    seeds = jax.random.split(jax.random.key(seed), 8)
    part_keys = jax.random.split(jax.random.fold_in(seeds[7], part), 8)
    train_acts = normal_values(part_keys[0], (MODULES, EXAMPLES, RANK, SEQ), 1.0, 6.0, ((0, 4), (1, 4)))
    train_grads = normal_values(part_keys[1], (MODULES, EXAMPLES, RANK, SEQ), 1.0, 6.0, ((0, 4), (1, 4)))
    lengths = plant(jax.random.randint(part_keys[2], (EXAMPLES,), SEQ // 4, SEQ + 1), jax.random.fold_in(part_keys[2], 1), SEQ // 4, SEQ).astype(jnp.int32)
    query_grads = normal_values(part_keys[3], (QUERIES, MODULES, RANK * RANK), (1.5 / (SEQ * MODULES * RANK * RANK) ** 0.5), 0.0078125, ((0, 4), (1, 4)))
    inv_in = draw_inv_in(jax.random.fold_in(seeds[7], 71), part)
    inv_out = draw_inv_out(jax.random.fold_in(seeds[7], 71), part)
    query_ids = plant(jax.random.randint(part_keys[6], (QUERIES,), 0, EXAMPLES), jax.random.fold_in(part_keys[6], 1), 0, EXAMPLES - 1).astype(jnp.int32)
    return dict(train_acts=train_acts, train_grads=train_grads, lengths=lengths, query_grads=query_grads, inv_in=inv_in, inv_out=inv_out, query_ids=query_ids)


def reference(train_acts, train_grads, lengths, query_grads, inv_in, inv_out, query_ids):
    positions = jnp.arange(SEQ, dtype=jnp.int32)
    keep_mask = (positions[None, :] < lengths[:, None]).astype(jnp.bfloat16)

    def one_module(blocks):
        act_block, grad_block = blocks
        masked = grad_block * keep_mask[:, None, :]
        outer_sum = jnp.einsum("not,nit->noi", masked.astype(jnp.float32), act_block.astype(jnp.float32))
        return outer_sum.astype(jnp.bfloat16).reshape(EXAMPLES, RANK * RANK)

    per_module = lax.map(one_module, (train_acts, train_grads))
    train_rows = jnp.transpose(per_module, (1, 0, 2)).reshape(EXAMPLES, MODULES * RANK * RANK)
    raw_queries = query_grads.astype(jnp.float32).reshape(QUERIES, MODULES, RANK, RANK)
    half_done = jnp.einsum("mab,qmbc->qmac", inv_out, raw_queries, precision=lax.Precision.HIGHEST)
    full_done = jnp.einsum("qmac,mcd->qmad", half_done, inv_in, precision=lax.Precision.HIGHEST)
    precond = full_done.astype(jnp.bfloat16).reshape(QUERIES, MODULES * RANK * RANK)
    scores = jnp.einsum("nk,qk->nq", train_rows.astype(jnp.float32), precond.astype(jnp.float32))
    example_index = jnp.arange(EXAMPLES, dtype=jnp.int32)
    same = example_index[:, None] == query_ids[None, :]
    return jnp.where(same, jnp.zeros_like(scores), scores)
```

```python
import functools

import jax
import jax.numpy as jnp
from jax import lax
from jax.experimental import pallas as pl
from jax.experimental.pallas import tpu as pltpu
from jax.sharding import PartitionSpec as P

MESH = pl.DeviceIdType.MESH
NT = (((1,), (1,)), ((), ()))
GROUP = 8


def iota(shape, dim):
    return lax.broadcasted_iota(jnp.int32, shape, dim)


def exact_dot(a, b):
    return jnp.dot(a, b, precision=lax.Precision.HIGHEST, preferred_element_type=jnp.float32)


def kernel(
    dp_size, layer_size, module_size,
    acts, grads, lengths, queries, inv_in, inv_out, ids,
    out,
    acts_v, grads_v, len_s, q_v, in_v, out_v, ids_v, q_flat, gathered, blocks, parts,
    load_sem, small_sem, send_sem, recv_sem, block_send, block_recv,
):
    mods, rows, seq = acts_v.shape
    rank = in_v.shape[1]
    ex = rows // rank
    width = rank * rank
    lm_size = layer_size * module_size
    groups = ex // GROUP
    grows = GROUP * rank
    local_q = q_v.shape[0]

    me = lax.axis_index("dp")
    lm = lax.axis_index("layer") * module_size + lax.axis_index("module")
    own_self = lm == me

    small = [
        pltpu.make_async_copy(lengths, len_s, small_sem.at[0]),
        pltpu.make_async_copy(inv_in, in_v, small_sem.at[1]),
        pltpu.make_async_copy(inv_out, out_v, small_sem.at[2]),
        pltpu.make_async_copy(ids, ids_v, small_sem.at[3]),
        pltpu.make_async_copy(queries, q_v, small_sem.at[4]),
    ]
    for copy in small[:4]:
        copy.start()
    loads = []
    for m in range(mods):
        for g in range(groups):
            part = pl.ds(g * grows, grows)
            k = m * groups + g
            pair = (
                pltpu.make_async_copy(grads.at[m, part], grads_v.at[m, part], load_sem.at[0, k]),
                pltpu.make_async_copy(acts.at[m, part], acts_v.at[m, part], load_sem.at[1, k]),
            )
            for copy in pair:
                copy.start()
            loads.append(pair)
    small[4].start()

    barrier = pltpu.get_barrier_semaphore()
    for k in range(1, dp_size):
        pl.semaphore_signal(
            barrier, inc=1, device_id={"dp": lax.rem(me + k, dp_size)}, device_id_type=MESH
        )
    for j in range(lm_size):
        @pl.when(jnp.logical_not(jnp.logical_and(own_self, lm == j)))
        def _(j=j):
            pl.semaphore_signal(
                barrier, inc=1,
                device_id={"dp": lm, "layer": j // module_size, "module": j % module_size},
                device_id_type=MESH,
            )

    for copy in small[:3]:
        copy.wait()
    spread_in = (iota((rank, 128), 0) == iota((rank, 128), 1) % rank).astype(jnp.float32)
    spread_out = (iota((rank, width), 0) == iota((rank, width), 1) // rank).astype(jnp.float32)
    block_diag = iota((grows, grows), 0) // rank == iota((grows, grows), 1) // rank
    positions = iota((1, seq), 1)
    right, left = [], []
    for m in range(mods):
        tiled = exact_dot(in_v[m], spread_in)
        high = tiled.astype(jnp.bfloat16)
        low = (tiled - high.astype(jnp.float32)).astype(jnp.bfloat16)
        both = jnp.concatenate([high, low], axis=1)
        right.append(jnp.concatenate([both] * GROUP, axis=0))
        left.append(exact_dot(out_v[m], spread_out))

    for m in range(mods):
        made = []
        for g in range(groups):
            for copy in loads[m * groups + g]:
                copy.wait()
            masked = []
            for n in range(GROUP):
                keep = (positions < len_s[g * GROUP + n]).astype(jnp.float32).astype(jnp.bfloat16)
                masked.append(grads_v[m, pl.ds(g * grows + n * rank, rank), :] * keep)
            outer = lax.dot_general(
                jnp.concatenate(masked, axis=0), acts_v[m, pl.ds(g * grows, grows), :], NT,
                preferred_element_type=jnp.float32,
            )
            diag = jnp.where(block_diag, outer, 0.0).astype(jnp.bfloat16)
            two = jnp.dot(diag, right[m], preferred_element_type=jnp.float32)
            half = (two[:, :128] + two[:, 128:]).reshape(GROUP, rank, 128)
            cols = []
            for c in range(width // 128):
                weight = left[m][:, c * 128:(c + 1) * 128]
                cols.append(jnp.sum(half * weight[None], axis=1))
            made.append(jnp.concatenate(cols, axis=1))
        gathered[m, me] = jnp.concatenate(made, axis=0).astype(jnp.bfloat16)
        if m == 0:
            pl.semaphore_wait(
                barrier, dp_size - 1 + dp_size - jnp.where(own_self, 1, 0)
            )
        for k in range(1, dp_size):
            to = lax.rem(me + k, dp_size)
            pltpu.make_async_remote_copy(
                src_ref=gathered.at[m, me], dst_ref=gathered.at[m, me],
                send_sem=send_sem.at[m, k], recv_sem=recv_sem.at[m, me],
                device_id={"dp": to}, device_id_type=MESH,
            ).start()

    small[3].wait()
    small[4].wait()
    q_flat[...] = q_v[...].reshape(local_q * mods, width)
    columns = local_q * mods
    parity = iota((1, columns), 1) % mods
    fold = (iota((columns, local_q), 0) // mods == iota((columns, local_q), 1)).astype(jnp.float32)

    def block_copy(slot, to):
        return pltpu.make_async_remote_copy(
            src_ref=blocks.at[slot], dst_ref=parts.at[lm],
            send_sem=block_send.at[slot], recv_sem=block_recv.at[lm],
            device_id={"dp": to, "layer": me // module_size, "module": me % module_size},
            device_id_type=MESH,
        )

    for k in range(dp_size):
        src = lax.rem(me + k, dp_size)
        total = None
        for m in range(mods):
            if k > 0:
                pltpu.make_async_remote_copy(
                    src_ref=gathered.at[m, src], dst_ref=gathered.at[m, src],
                    send_sem=send_sem.at[m, k], recv_sem=recv_sem.at[m, src],
                    device_id={"dp": src}, device_id_type=MESH,
                ).wait_recv()
            score = lax.dot_general(
                gathered[m, src], q_flat[...], NT, preferred_element_type=jnp.float32
            )
            total = score if total is None else jnp.where(parity == m, score, total)
        total = exact_dot(total, fold)
        if k == 0:
            @pl.when(own_self)
            def _():
                parts[lm] = total

            @pl.when(jnp.logical_not(own_self))
            def _():
                blocks[0] = total
                block_copy(0, src).start()
        else:
            blocks[k] = total
            block_copy(k, src).start()

    for j in range(lm_size):
        @pl.when(jnp.logical_not(jnp.logical_and(own_self, lm == j)))
        def _(j=j):
            pltpu.make_async_remote_copy(
                src_ref=blocks.at[0], dst_ref=parts.at[j],
                send_sem=block_send.at[0], recv_sem=block_recv.at[j],
                device_id={"dp": lm, "layer": j // module_size, "module": j % module_size},
                device_id_type=MESH,
            ).wait_recv()
    total = parts[0]
    for j in range(1, lm_size):
        total = total + parts[j]
    owned = ids_v[:, :local_q]
    for j in range(1, lm_size):
        owned = jnp.where(lm == j, ids_v[:, j * local_q:(j + 1) * local_q], owned)
    same = me * ex + iota((ex, local_q), 0) == owned
    out[...] = jnp.where(same, 0.0, total)

    for m in range(mods):
        for k in range(1, dp_size):
            pltpu.make_async_remote_copy(
                src_ref=gathered.at[m, me], dst_ref=gathered.at[m, me],
                send_sem=send_sem.at[m, k], recv_sem=recv_sem.at[m, me],
                device_id={"dp": lax.rem(me + k, dp_size)}, device_id_type=MESH,
            ).wait_send()
    for k in range(dp_size):
        if k == 0:
            @pl.when(jnp.logical_not(own_self))
            def _():
                block_copy(0, me).wait_send()
        else:
            block_copy(k, lax.rem(me + k, dp_size)).wait_send()


def on_device(sizes, train_acts, train_grads, lengths, query_grads, inv_in, inv_out, query_ids):
    dp_size, layer_size, module_size = sizes
    mods, ex, rank, seq = train_acts.shape
    local_q, _, width = query_grads.shape
    lm_size = layer_size * module_size
    rows = ex * rank
    chunks = mods * (ex // GROUP)
    anywhere = pl.BlockSpec(memory_space=pl.ANY)
    return pl.pallas_call(
        functools.partial(kernel, dp_size, layer_size, module_size),
        out_shape=jax.ShapeDtypeStruct((ex, local_q), jnp.float32),
        in_specs=[anywhere] * 7,
        out_specs=pl.BlockSpec(memory_space=pltpu.VMEM),
        scratch_shapes=[
            pltpu.VMEM((mods, rows, seq), jnp.bfloat16),
            pltpu.VMEM((mods, rows, seq), jnp.bfloat16),
            pltpu.SMEM((ex,), jnp.int32),
            pltpu.VMEM((local_q, mods, width), jnp.bfloat16),
            pltpu.VMEM((mods, rank, rank), jnp.float32),
            pltpu.VMEM((mods, rank, rank), jnp.float32),
            pltpu.VMEM((1, query_ids.shape[0]), jnp.int32),
            pltpu.VMEM((local_q * mods, width), jnp.bfloat16),
            pltpu.VMEM((mods, dp_size, ex, width), jnp.bfloat16),
            pltpu.VMEM((dp_size, ex, local_q), jnp.float32),
            pltpu.VMEM((lm_size, ex, local_q), jnp.float32),
            pltpu.SemaphoreType.DMA((2, chunks)),
            pltpu.SemaphoreType.DMA((5,)),
            pltpu.SemaphoreType.DMA((mods, dp_size)),
            pltpu.SemaphoreType.DMA((mods, dp_size)),
            pltpu.SemaphoreType.DMA((dp_size,)),
            pltpu.SemaphoreType.DMA((lm_size,)),
        ],
        compiler_params=pltpu.CompilerParams(
            collective_id=0, has_side_effects=True, vmem_limit_bytes=48 * 1024 * 1024
        ),
    )(
        train_acts.reshape(mods, rows, seq),
        train_grads.reshape(mods, rows, seq),
        lengths, query_grads, inv_in, inv_out,
        query_ids.reshape(1, -1),
    )


def solution(mesh):
    sizes = tuple(mesh.shape[name] for name in ("dp", "layer", "module"))
    assert sizes[0] == sizes[1] * sizes[2]
    return jax.shard_map(
        functools.partial(on_device, sizes),
        mesh=mesh,
        in_specs=(
            P(("layer", "module"), ("parts", "dp"), None, None),
            P(("layer", "module"), ("parts", "dp"), None, None),
            P(("parts", "dp")),
            P(("parts", "dp"), ("layer", "module"), None),
            P(("layer", "module"), None, None),
            P(("layer", "module"), None, None),
            P("parts"),
        ),
        out_specs=P(("parts", "dp"), ("layer", "module")),
        check_vma=False,
    )
```

```python
import functools

import jax
import jax.numpy as jnp
from jax import lax
from jax.experimental import pallas as pl
from jax.experimental.pallas import tpu as pltpu
from jax.sharding import PartitionSpec as P

MESH = pl.DeviceIdType.MESH
NT = (((1,), (1,)), ((), ()))
GROUP = 8


def iota(shape, dim):
    return lax.broadcasted_iota(jnp.int32, shape, dim)


def plain_dot(a, b):
    return jnp.dot(a, b, preferred_element_type=jnp.float32)


def terms(x):
    high = x.astype(jnp.bfloat16)
    rest = x - high.astype(jnp.float32)
    middle = rest.astype(jnp.bfloat16)
    return high, middle, (rest - middle.astype(jnp.float32)).astype(jnp.bfloat16)


def kernel(
    dp_size, layer_size, module_size,
    acts, grads, lengths, queries, inv_in, inv_out, ids,
    out,
    acts_v, grads_v, len_s, q_v, in_v, out_v, ids_v, right, left, q_t, gathered, blocks, parts,
    load_sem, small_sem, send_sem, recv_sem, block_send, block_recv,
):
    mods, rows, seq = acts_v.shape
    rank = in_v.shape[1]
    ex = rows // rank
    width = rank * rank
    lm_size = layer_size * module_size
    groups = ex // GROUP
    grows = GROUP * rank
    local_q = q_v.shape[0]

    me = lax.axis_index("dp")
    lm = lax.axis_index("layer") * module_size + lax.axis_index("module")
    own_self = lm == me
    upper = 2 * me >= dp_size

    def peer(i):
        down = dp_size - 1 - i
        up = jnp.where(me <= i, i + 1, i)
        return jnp.where(upper, up, jnp.where(down <= me, down - 1, down))

    small = [
        pltpu.make_async_copy(lengths, len_s, small_sem.at[0]),
        pltpu.make_async_copy(inv_in, in_v, small_sem.at[1]),
        pltpu.make_async_copy(inv_out, out_v, small_sem.at[2]),
        pltpu.make_async_copy(ids, ids_v, small_sem.at[3]),
        pltpu.make_async_copy(queries, q_v, small_sem.at[4]),
    ]
    for copy in small[:4]:
        copy.start()

    def load_copy(pair, m, g):
        part = pl.ds(pl.multiple_of(g * grows, grows), grows)
        source, target = ((grads, grads_v), (acts, acts_v))[pair]
        return pltpu.make_async_copy(
            source.at[m, part], target.at[m, part], load_sem.at[pair, m, g]
        )

    for m in range(mods):
        for g in range(groups):
            for pair in range(2):
                load_copy(pair, m, g).start()
    small[4].start()

    barrier = pltpu.get_barrier_semaphore()
    for k in range(1, dp_size):
        pl.semaphore_signal(
            barrier, inc=1, device_id={"dp": lax.rem(me + k, dp_size)}, device_id_type=MESH
        )
    for j in range(lm_size):
        @pl.when(jnp.logical_not(jnp.logical_and(own_self, lm == j)))
        def _(j=j):
            pl.semaphore_signal(
                barrier, inc=1,
                device_id={"dp": lm, "layer": j // module_size, "module": j % module_size},
                device_id_type=MESH,
            )

    half = width // 2

    def rows_copy(m, g, owner, slot, to):
        place = gathered.at[m, owner, pl.ds(pl.multiple_of(g * 2 * GROUP, 2 * GROUP), 2 * GROUP)]
        return pltpu.make_async_remote_copy(
            src_ref=place, dst_ref=place,
            send_sem=send_sem.at[m, g, slot], recv_sem=recv_sem.at[m, g, owner],
            device_id={"dp": to}, device_id_type=MESH,
        )

    def loop(count, body):
        def step(i, carry):
            body(i)
            return carry

        lax.fori_loop(0, count, step, 0)

    for copy in small[:3]:
        copy.wait()
    spread_in = (iota((rank, 128), 0) == iota((rank, 128), 1) % rank).astype(jnp.bfloat16)
    spread_out = (iota((rank, width), 0) == iota((rank, width), 1) // rank).astype(jnp.bfloat16)
    positions = iota((1, seq), 1)

    def set_up(m):
        high, low, _ = terms(in_v[m])
        both = jnp.concatenate([plain_dot(high, spread_in), plain_dot(low, spread_in)], axis=1)
        right[m] = jnp.concatenate([both.astype(jnp.bfloat16)] * GROUP, axis=0)
        left[m] = sum(plain_dot(term, spread_out) for term in terms(out_v[m]))

    loop(mods, set_up)

    def chunk(c):
        m, g = c // groups, c % groups
        start = pl.multiple_of(g * grows, grows)
        for pair in range(2):
            load_copy(pair, m, g).wait()
        masked = []
        for n in range(GROUP):
            keep = (positions < len_s[g * GROUP + n]).astype(jnp.float32).astype(jnp.bfloat16)
            masked.append(grads_v[m, pl.ds(start + n * rank, rank), :] * keep)
        outer = lax.dot_general(
            jnp.concatenate(masked, axis=0), acts_v[m, pl.ds(start, grows), :], NT,
            preferred_element_type=jnp.float32,
        )
        block_diag = iota((grows, grows), 0) // rank == iota((grows, grows), 1) // rank
        diag = jnp.where(block_diag, outer, 0.0).astype(jnp.bfloat16)
        two = plain_dot(diag, right[m])
        one = (two[:, :128] + two[:, 128:]).reshape(GROUP, rank, 128)
        cols = []
        for col in range(width // 128):
            weight = left[m, :, col * 128:(col + 1) * 128]
            cols.append(jnp.sum(one * weight[None], axis=1))
        made = jnp.concatenate(cols, axis=1)
        gathered[m, me, pl.ds(pl.multiple_of(g * 2 * GROUP, 2 * GROUP), 2 * GROUP)] = (
            jnp.concatenate([made[:, :half], made[:, half:]], axis=0).astype(jnp.bfloat16)
        )

        @pl.when(c == 0)
        def _():
            pl.semaphore_wait(barrier, dp_size - 1 + dp_size - jnp.where(own_self, 1, 0))

        for i in range(dp_size - 1):
            rows_copy(m, g, me, i, peer(i)).start()

    loop(mods * groups, chunk)

    small[3].wait()
    small[4].wait()
    columns = local_q * mods

    def prepare(m):
        pick = iota((local_q, columns), 1) == iota((local_q, columns), 0) * mods + m
        chosen = plain_dot(pick.astype(jnp.bfloat16), q_v[...].reshape(columns, width))
        q_t[m] = chosen.T.astype(jnp.bfloat16)

    loop(mods, prepare)

    def block_copy(slot, sender, to):
        return pltpu.make_async_remote_copy(
            src_ref=blocks.at[slot], dst_ref=parts.at[sender],
            send_sem=block_send.at[slot], recv_sem=block_recv.at[sender],
            device_id={"dp": to, "layer": me // module_size, "module": me % module_size},
            device_id_type=MESH,
        )

    def source(k):
        return jnp.where(k == 0, me, peer(dp_size - 1 - k))

    def score(k):
        src = source(k)

        @pl.when(k > 0)
        def _():
            for m in range(mods):
                for g in range(groups):
                    rows_copy(m, g, src, 0, src).wait_recv()

        sides = [
            sum(plain_dot(gathered[m, src], q_t[m, side]) for m in range(mods))
            for side in (pl.ds(0, half), pl.ds(half, half))
        ]
        total = jnp.concatenate([
            sides[0][2 * g * GROUP:(2 * g + 1) * GROUP]
            + sides[1][(2 * g + 1) * GROUP:(2 * g + 2) * GROUP]
            for g in range(groups)
        ], axis=0)
        stays = jnp.logical_and(own_self, k == 0)

        @pl.when(stays)
        def _():
            parts[lm] = total

        @pl.when(jnp.logical_not(stays))
        def _():
            blocks[k] = total
            block_copy(k, lm, src).start()

    loop(dp_size, score)

    def collect(j):
        @pl.when(jnp.logical_not(jnp.logical_and(own_self, lm == j)))
        def _():
            block_copy(0, j, lm).wait_recv()

    loop(lm_size, collect)
    total = parts[0]
    for j in range(1, lm_size):
        total = total + parts[j]
    owned = ids_v[:, :local_q]
    for j in range(1, lm_size):
        owned = jnp.where(lm == j, ids_v[:, j * local_q:(j + 1) * local_q], owned)
    same = me * ex + iota((ex, local_q), 0) == owned
    out[...] = jnp.where(same, 0.0, total)

    def sent(i):
        for m in range(mods):
            for g in range(groups):
                rows_copy(m, g, me, i, peer(i)).wait_send()

    loop(dp_size - 1, sent)

    def block_sent(k):
        @pl.when(jnp.logical_not(jnp.logical_and(own_self, k == 0)))
        def _():
            block_copy(k, lm, source(k)).wait_send()

    loop(dp_size, block_sent)


def on_device(sizes, train_acts, train_grads, lengths, query_grads, inv_in, inv_out, query_ids):
    dp_size, layer_size, module_size = sizes
    mods, ex, rank, seq = train_acts.shape
    local_q, _, width = query_grads.shape
    lm_size = layer_size * module_size
    rows = ex * rank
    anywhere = pl.BlockSpec(memory_space=pltpu.HBM)
    return pl.pallas_call(
        functools.partial(kernel, dp_size, layer_size, module_size),
        out_shape=jax.ShapeDtypeStruct((ex, local_q), jnp.float32),
        in_specs=[anywhere] * 7,
        out_specs=pl.BlockSpec(memory_space=pltpu.VMEM),
        scratch_shapes=[
            pltpu.VMEM((mods, rows, seq), jnp.bfloat16),
            pltpu.VMEM((mods, rows, seq), jnp.bfloat16),
            pltpu.SMEM((ex,), jnp.int32),
            pltpu.VMEM((local_q, mods, width), jnp.bfloat16),
            pltpu.VMEM((mods, rank, rank), jnp.float32),
            pltpu.VMEM((mods, rank, rank), jnp.float32),
            pltpu.VMEM((1, query_ids.shape[0]), jnp.int32),
            pltpu.VMEM((mods, GROUP * rank, 256), jnp.bfloat16),
            pltpu.VMEM((mods, rank, width), jnp.float32),
            pltpu.VMEM((mods, width, local_q), jnp.bfloat16),
            pltpu.VMEM((mods, dp_size, 2 * ex, width // 2), jnp.bfloat16),
            pltpu.VMEM((dp_size, ex, local_q), jnp.float32),
            pltpu.VMEM((lm_size, ex, local_q), jnp.float32),
            pltpu.SemaphoreType.DMA((2, mods, ex // GROUP)),
            pltpu.SemaphoreType.DMA((5,)),
            pltpu.SemaphoreType.DMA((mods, ex // GROUP, dp_size)),
            pltpu.SemaphoreType.DMA((mods, ex // GROUP, dp_size)),
            pltpu.SemaphoreType.DMA((dp_size,)),
            pltpu.SemaphoreType.DMA((lm_size,)),
        ],
        compiler_params=pltpu.CompilerParams(
            collective_id=0, has_side_effects=True, vmem_limit_bytes=60 * 1024 * 1024
        ),
    )(
        train_acts.reshape(mods, rows, seq),
        train_grads.reshape(mods, rows, seq),
        lengths, query_grads, inv_in, inv_out,
        query_ids.reshape(1, -1),
    )


def solution(mesh):
    sizes = tuple(mesh.shape[name] for name in ("dp", "layer", "module"))
    assert sizes[0] == sizes[1] * sizes[2]
    return jax.shard_map(
        functools.partial(on_device, sizes),
        mesh=mesh,
        in_specs=(
            P(("layer", "module"), ("parts", "dp"), None, None),
            P(("layer", "module"), ("parts", "dp"), None, None),
            P(("parts", "dp")),
            P(("parts", "dp"), ("layer", "module"), None),
            P(("layer", "module"), None, None),
            P(("layer", "module"), None, None),
            P("parts"),
        ),
        out_specs=P(("parts", "dp"), ("layer", "module")),
        check_vma=False,
    )
```

```python
import functools

import jax
import jax.numpy as jnp
from jax import lax
from jax.experimental import pallas as pl
from jax.experimental.pallas import tpu as pltpu
from jax.sharding import PartitionSpec as P

MESH = pl.DeviceIdType.MESH
NT = (((1,), (1,)), ((), ()))
GROUP = 8


def iota(shape, dim):
    return lax.broadcasted_iota(jnp.int32, shape, dim)


def plain_dot(a, b):
    return jnp.dot(a, b, preferred_element_type=jnp.float32)


def terms(x):
    high = x.astype(jnp.bfloat16)
    rest = x - high.astype(jnp.float32)
    middle = rest.astype(jnp.bfloat16)
    return high, middle, (rest - middle.astype(jnp.float32)).astype(jnp.bfloat16)


def kernel(
    dp_size, layer_size, module_size,
    acts, grads, lengths, queries, inv_in, inv_out, ids,
    out,
    acts_v, grads_v, len_s, q_v, in_v, out_v, ids_v, right, left, q_t, gathered, blocks, parts,
    load_sem, small_sem, send_sem, recv_sem, block_send, block_recv,
):
    mods, rows, seq = acts_v.shape
    rank = in_v.shape[1]
    ex = rows // rank
    width = rank * rank
    lm_size = layer_size * module_size
    groups = ex // GROUP
    grows = GROUP * rank
    local_q = q_v.shape[0]

    me = lax.axis_index("dp")
    lm = lax.axis_index("layer") * module_size + lax.axis_index("module")
    own_self = lm == me
    upper = 2 * me >= dp_size

    def peer(i):
        down = dp_size - 1 - i
        up = jnp.where(me <= i, i + 1, i)
        return jnp.where(upper, up, jnp.where(down <= me, down - 1, down))

    barrier = pltpu.get_barrier_semaphore()
    for k in range(1, dp_size):
        pl.semaphore_signal(
            barrier, inc=1, device_id={"dp": lax.rem(me + k, dp_size)}, device_id_type=MESH
        )
    for j in range(lm_size):
        @pl.when(jnp.logical_not(jnp.logical_and(own_self, lm == j)))
        def _(j=j):
            pl.semaphore_signal(
                barrier, inc=1,
                device_id={"dp": lm, "layer": j // module_size, "module": j % module_size},
                device_id_type=MESH,
            )

    half = width // 2

    def rows_copy(m, owner, slot, to):
        place = gathered.at[m, owner]
        return pltpu.make_async_remote_copy(
            src_ref=place, dst_ref=place,
            send_sem=send_sem.at[m, slot], recv_sem=recv_sem.at[m, owner],
            device_id={"dp": to}, device_id_type=MESH,
        )

    def loop(count, body):
        def step(i, carry):
            body(i)
            return carry

        lax.fori_loop(0, count, step, 0)

    small = [
        pltpu.make_async_copy(lengths, len_s, small_sem.at[0]),
        pltpu.make_async_copy(inv_in, in_v, small_sem.at[1]),
        pltpu.make_async_copy(inv_out, out_v, small_sem.at[2]),
        pltpu.make_async_copy(ids, ids_v, small_sem.at[3]),
        pltpu.make_async_copy(queries, q_v, small_sem.at[4]),
    ]

    def load_copy(pair, m, g):
        part = pl.ds(pl.multiple_of(g * grows, grows), grows)
        source, target = ((grads, grads_v), (acts, acts_v))[pair]
        return pltpu.make_async_copy(
            source.at[m, part], target.at[m, part], load_sem.at[pair, m, g]
        )

    def load(m):
        for g in range(groups):
            for pair in range(2):
                load_copy(pair, m, g).start()

    load(0)
    for copy in small[:4]:
        copy.start()

    for copy in small[:3]:
        copy.wait()
    spread_in = (iota((rank, 128), 0) == iota((rank, 128), 1) % rank).astype(jnp.bfloat16)
    spread_out = (iota((rank, width), 0) == iota((rank, width), 1) // rank).astype(jnp.bfloat16)
    positions = iota((1, seq), 1)

    def set_up(m):
        high, low, _ = terms(in_v[m])
        both = jnp.concatenate([plain_dot(high, spread_in), plain_dot(low, spread_in)], axis=1)
        right[m] = jnp.concatenate([both.astype(jnp.bfloat16)] * GROUP, axis=0)
        left[m] = sum(plain_dot(term, spread_out) for term in terms(out_v[m]))

    for m in range(1, mods):
        load(m)

    loop(mods, set_up)

    block_diag = iota((grows, grows), 0) // rank == iota((grows, grows), 1) // rank

    def rows_of(m, g):
        start = g * grows
        masked = []
        for n in range(GROUP):
            keep = (positions < len_s[g * GROUP + n]).astype(jnp.float32).astype(jnp.bfloat16)
            masked.append(grads_v[m, pl.ds(start + n * rank, rank), :] * keep)
        outer = lax.dot_general(
            jnp.concatenate(masked, axis=0), acts_v[m, pl.ds(start, grows), :], NT,
            preferred_element_type=jnp.float32,
        )
        diag = jnp.where(block_diag, outer, 0.0).astype(jnp.bfloat16)
        two = plain_dot(diag, right[m])
        one = (two[:, :128] + two[:, 128:]).reshape(GROUP, rank, 128)
        cols = []
        for col in range(width // 128):
            weight = left[m, :, col * 128:(col + 1) * 128]
            cols.append(jnp.sum(one * weight[None], axis=1))
        made = jnp.concatenate(cols, axis=1)
        return jnp.concatenate([made[:, :half], made[:, half:]], axis=0).astype(jnp.bfloat16)

    def module_rows(m):
        for g in range(groups):
            for pair in range(2):
                load_copy(pair, m, g).wait()
        gathered[m, me] = jnp.concatenate([rows_of(m, g) for g in range(groups)], axis=0)

        @pl.when(m == 0)
        def _():
            small[4].start()
            pl.semaphore_wait(barrier, dp_size - 1 + dp_size - jnp.where(own_self, 1, 0))

        for i in range(dp_size - 1):
            rows_copy(m, me, i, peer(i)).start()

    loop(mods, module_rows)

    small[3].wait()
    small[4].wait()
    columns = local_q * mods

    def prepare(m):
        pick = iota((local_q, columns), 1) == iota((local_q, columns), 0) * mods + m
        chosen = plain_dot(pick.astype(jnp.bfloat16), q_v[...].reshape(columns, width))
        q_t[m] = chosen.T.astype(jnp.bfloat16)

    loop(mods, prepare)

    def block_copy(slot, sender, to):
        return pltpu.make_async_remote_copy(
            src_ref=blocks.at[slot], dst_ref=parts.at[sender],
            send_sem=block_send.at[slot], recv_sem=block_recv.at[sender],
            device_id={"dp": to, "layer": me // module_size, "module": me % module_size},
            device_id_type=MESH,
        )

    def source(k):
        return jnp.where(k == 0, me, peer(dp_size - 1 - k))

    def score(k):
        src = source(k)

        @pl.when(k > 0)
        def _():
            for m in range(mods):
                rows_copy(m, src, 0, src).wait_recv()

        sides = [
            sum(plain_dot(gathered[m, src], q_t[m, side]) for m in range(mods))
            for side in (pl.ds(0, half), pl.ds(half, half))
        ]
        total = jnp.concatenate([
            sides[0][2 * g * GROUP:(2 * g + 1) * GROUP]
            + sides[1][(2 * g + 1) * GROUP:(2 * g + 2) * GROUP]
            for g in range(groups)
        ], axis=0)
        stays = jnp.logical_and(own_self, k == 0)

        @pl.when(stays)
        def _():
            parts[lm] = total

        @pl.when(jnp.logical_not(stays))
        def _():
            blocks[k] = total
            block_copy(k, lm, src).start()

    loop(dp_size, score)

    def collect(j):
        @pl.when(jnp.logical_not(jnp.logical_and(own_self, lm == j)))
        def _():
            block_copy(0, j, lm).wait_recv()

    loop(lm_size, collect)
    total = parts[0]
    for j in range(1, lm_size):
        total = total + parts[j]
    owned = ids_v[:, :local_q]
    for j in range(1, lm_size):
        owned = jnp.where(lm == j, ids_v[:, j * local_q:(j + 1) * local_q], owned)
    same = me * ex + iota((ex, local_q), 0) == owned
    out[...] = jnp.where(same, 0.0, total)

    def sent(i):
        for m in range(mods):
            rows_copy(m, me, i, peer(i)).wait_send()

    loop(dp_size - 1, sent)

    def block_sent(k):
        @pl.when(jnp.logical_not(jnp.logical_and(own_self, k == 0)))
        def _():
            block_copy(k, lm, source(k)).wait_send()

    loop(dp_size, block_sent)


def on_device(sizes, train_acts, train_grads, lengths, query_grads, inv_in, inv_out, query_ids):
    dp_size, layer_size, module_size = sizes
    mods, ex, rank, seq = train_acts.shape
    local_q, _, width = query_grads.shape
    lm_size = layer_size * module_size
    rows = ex * rank
    anywhere = pl.BlockSpec(memory_space=pltpu.HBM)
    return pl.pallas_call(
        functools.partial(kernel, dp_size, layer_size, module_size),
        out_shape=jax.ShapeDtypeStruct((ex, local_q), jnp.float32),
        in_specs=[anywhere] * 7,
        out_specs=pl.BlockSpec(memory_space=pltpu.VMEM),
        scratch_shapes=[
            pltpu.VMEM((mods, rows, seq), jnp.bfloat16),
            pltpu.VMEM((mods, rows, seq), jnp.bfloat16),
            pltpu.SMEM((ex,), jnp.int32),
            pltpu.VMEM((local_q, mods, width), jnp.bfloat16),
            pltpu.VMEM((mods, rank, rank), jnp.float32),
            pltpu.VMEM((mods, rank, rank), jnp.float32),
            pltpu.VMEM((1, query_ids.shape[0]), jnp.int32),
            pltpu.VMEM((mods, GROUP * rank, 256), jnp.bfloat16),
            pltpu.VMEM((mods, rank, width), jnp.float32),
            pltpu.VMEM((mods, width, local_q), jnp.bfloat16),
            pltpu.VMEM((mods, dp_size, 2 * ex, width // 2), jnp.bfloat16),
            pltpu.VMEM((dp_size, ex, local_q), jnp.float32),
            pltpu.VMEM((lm_size, ex, local_q), jnp.float32),
            pltpu.SemaphoreType.DMA((2, mods, ex // GROUP)),
            pltpu.SemaphoreType.DMA((5,)),
            pltpu.SemaphoreType.DMA((mods, dp_size)),
            pltpu.SemaphoreType.DMA((mods, dp_size)),
            pltpu.SemaphoreType.DMA((dp_size,)),
            pltpu.SemaphoreType.DMA((lm_size,)),
        ],
        compiler_params=pltpu.CompilerParams(
            collective_id=0, has_side_effects=True, vmem_limit_bytes=60 * 1024 * 1024
        ),
    )(
        train_acts.reshape(mods, rows, seq),
        train_grads.reshape(mods, rows, seq),
        lengths, query_grads, inv_in, inv_out,
        query_ids.reshape(1, -1),
    )


def solution(mesh):
    sizes = tuple(mesh.shape[name] for name in ("dp", "layer", "module"))
    assert sizes[0] == sizes[1] * sizes[2]
    return jax.shard_map(
        functools.partial(on_device, sizes),
        mesh=mesh,
        in_specs=(
            P(("layer", "module"), ("parts", "dp"), None, None),
            P(("layer", "module"), ("parts", "dp"), None, None),
            P(("parts", "dp")),
            P(("parts", "dp"), ("layer", "module"), None),
            P(("layer", "module"), None, None),
            P(("layer", "module"), None, None),
            P("parts"),
        ),
        out_specs=P(("parts", "dp"), ("layer", "module")),
        check_vma=False,
    )
```

```python
import functools

import jax
import jax.numpy as jnp
from jax import lax
from jax.experimental import pallas as pl
from jax.experimental.pallas import tpu as pltpu
from jax.sharding import PartitionSpec as P

MESH = pl.DeviceIdType.MESH
NT = (((1,), (1,)), ((), ()))
GROUP = 8


def iota(shape, dim):
    return lax.broadcasted_iota(jnp.int32, shape, dim)


def plain_dot(a, b):
    return jnp.dot(a, b, preferred_element_type=jnp.float32)


def terms(x):
    high = x.astype(jnp.bfloat16)
    rest = x - high.astype(jnp.float32)
    middle = rest.astype(jnp.bfloat16)
    return high, middle, (rest - middle.astype(jnp.float32)).astype(jnp.bfloat16)


def kernel(
    dp_size, layer_size, module_size,
    acts, grads, lengths, queries, inv_in, inv_out, ids,
    out,
    acts_v, grads_v, len_s, q_v, in_v, out_v, ids_v, right, left, q_t, held, gathered, blocks, parts,
    load_sem, small_sem, send_sem, recv_sem, block_send, block_recv,
):
    mods, rows, seq = acts_v.shape
    rank = in_v.shape[1]
    ex = rows // rank
    width = rank * rank
    lm_size = layer_size * module_size
    groups = ex // GROUP
    grows = GROUP * rank
    local_q = q_v.shape[0]

    me = lax.axis_index("dp")
    lm = lax.axis_index("layer") * module_size + lax.axis_index("module")
    own_self = lm == me
    upper = 2 * me >= dp_size

    def peer(i):
        down = dp_size - 1 - i
        up = jnp.where(me <= i, i + 1, i)
        return jnp.where(upper, up, jnp.where(down <= me, down - 1, down))

    barrier = pltpu.get_barrier_semaphore()
    for k in range(1, dp_size):
        pl.semaphore_signal(
            barrier, inc=1, device_id={"dp": lax.rem(me + k, dp_size)}, device_id_type=MESH
        )
    for j in range(lm_size):
        @pl.when(jnp.logical_not(jnp.logical_and(own_self, lm == j)))
        def _(j=j):
            pl.semaphore_signal(
                barrier, inc=1,
                device_id={"dp": lm, "layer": j // module_size, "module": j % module_size},
                device_id_type=MESH,
            )

    half = width // 2

    def rows_copy(m, owner, slot, to):
        place = gathered.at[m, owner]
        return pltpu.make_async_remote_copy(
            src_ref=place, dst_ref=place,
            send_sem=send_sem.at[m, slot], recv_sem=recv_sem.at[m, owner],
            device_id={"dp": to}, device_id_type=MESH,
        )

    def loop(count, body):
        def step(i, carry):
            body(i)
            return carry

        lax.fori_loop(0, count, step, 0)

    small = [
        pltpu.make_async_copy(lengths, len_s, small_sem.at[0]),
        pltpu.make_async_copy(inv_in, in_v, small_sem.at[1]),
        pltpu.make_async_copy(inv_out, out_v, small_sem.at[2]),
        pltpu.make_async_copy(ids, ids_v, small_sem.at[3]),
        pltpu.make_async_copy(queries, q_v, small_sem.at[4]),
    ]

    def load_copy(pair, m, g):
        part = pl.ds(pl.multiple_of(g * grows, grows), grows)
        source, target = ((grads, grads_v), (acts, acts_v))[pair]
        return pltpu.make_async_copy(
            source.at[m, part], target.at[m, part], load_sem.at[pair, m, g]
        )

    def load(m):
        for g in range(groups):
            for pair in range(2):
                load_copy(pair, m, g).start()

    load(0)
    for copy in small[:4]:
        copy.start()

    for copy in small[:3]:
        copy.wait()
    spread_in = (iota((rank, 128), 0) == iota((rank, 128), 1) % rank).astype(jnp.bfloat16)
    spread_out = (iota((rank, width), 0) == iota((rank, width), 1) // rank).astype(jnp.bfloat16)
    positions = iota((1, seq), 1)

    def set_up(m):
        high, low, _ = terms(in_v[m])
        both = jnp.concatenate([plain_dot(high, spread_in), plain_dot(low, spread_in)], axis=1)
        right[m] = jnp.concatenate([both.astype(jnp.bfloat16)] * GROUP, axis=0)
        left[m] = sum(plain_dot(term, spread_out) for term in terms(out_v[m]))

    for m in range(1, mods):
        load(m)

    loop(mods, set_up)

    block_diag = iota((grows, grows), 0) // rank == iota((grows, grows), 1) // rank

    def rows_of(m, g):
        start = g * grows
        masked = []
        for n in range(GROUP):
            keep = (positions < len_s[g * GROUP + n]).astype(jnp.float32).astype(jnp.bfloat16)
            masked.append(grads_v[m, pl.ds(start + n * rank, rank), :] * keep)
        outer = lax.dot_general(
            jnp.concatenate(masked, axis=0), acts_v[m, pl.ds(start, grows), :], NT,
            preferred_element_type=jnp.float32,
        )
        diag = jnp.where(block_diag, outer, 0.0).astype(jnp.bfloat16)
        two = plain_dot(diag, right[m])
        one = (two[:, :128] + two[:, 128:]).reshape(GROUP, rank, 128)
        cols = []
        for col in range(width // 128):
            weight = left[m, :, col * 128:(col + 1) * 128]
            cols.append(jnp.sum(one * weight[None], axis=1))
        made = jnp.concatenate(cols, axis=1)
        return jnp.concatenate([made[:, :half], made[:, half:]], axis=0).astype(jnp.bfloat16)

    def module_rows(m):
        for g in range(groups):
            for pair in range(2):
                load_copy(pair, m, g).wait()
        gathered[m, me] = jnp.concatenate([rows_of(m, g) for g in range(groups)], axis=0)

        @pl.when(m == 0)
        def _():
            small[4].start()
            pl.semaphore_wait(barrier, dp_size - 1 + dp_size - jnp.where(own_self, 1, 0))

        for i in range(dp_size - 1):
            rows_copy(m, me, i, peer(i)).start()

    loop(mods, module_rows)

    small[3].wait()
    small[4].wait()
    columns = local_q * mods

    def prepare(m):
        pick = iota((local_q, columns), 1) == iota((local_q, columns), 0) * mods + m
        chosen = plain_dot(pick.astype(jnp.bfloat16), q_v[...].reshape(columns, width))
        q_t[m] = chosen.T.astype(jnp.bfloat16)

    loop(mods, prepare)

    def block_copy(slot, sender, to):
        return pltpu.make_async_remote_copy(
            src_ref=blocks.at[slot], dst_ref=parts.at[sender],
            send_sem=block_send.at[slot], recv_sem=block_recv.at[sender],
            device_id={"dp": to, "layer": me // module_size, "module": me % module_size},
            device_id_type=MESH,
        )

    def source(k):
        return jnp.where(k == 0, me, peer(dp_size - 1 - k))

    def early(k):
        src = source(k)

        @pl.when(k > 0)
        def _():
            for m in range(mods - 1):
                rows_copy(m, src, 0, src).wait_recv()

        for side in range(2):
            held[side, k] = sum(
                plain_dot(gathered[m, src], q_t[m, pl.ds(side * half, half)])
                for m in range(mods - 1)
            )

    loop(dp_size, early)

    def score(k):
        src = source(k)

        @pl.when(k > 0)
        def _():
            rows_copy(mods - 1, src, 0, src).wait_recv()

        sides = [
            held[side, k] + plain_dot(gathered[mods - 1, src], q_t[mods - 1, pl.ds(side * half, half)])
            for side in range(2)
        ]
        total = jnp.concatenate([
            sides[0][2 * g * GROUP:(2 * g + 1) * GROUP]
            + sides[1][(2 * g + 1) * GROUP:(2 * g + 2) * GROUP]
            for g in range(groups)
        ], axis=0)
        stays = jnp.logical_and(own_self, k == 0)

        @pl.when(stays)
        def _():
            parts[lm] = total

        @pl.when(jnp.logical_not(stays))
        def _():
            blocks[k] = total
            block_copy(k, lm, src).start()

    loop(dp_size, score)

    def collect(j):
        @pl.when(jnp.logical_not(jnp.logical_and(own_self, lm == j)))
        def _():
            block_copy(0, j, lm).wait_recv()

    loop(lm_size, collect)
    total = parts[0]
    for j in range(1, lm_size):
        total = total + parts[j]
    owned = ids_v[:, :local_q]
    for j in range(1, lm_size):
        owned = jnp.where(lm == j, ids_v[:, j * local_q:(j + 1) * local_q], owned)
    same = me * ex + iota((ex, local_q), 0) == owned
    out[...] = jnp.where(same, 0.0, total)

    def sent(i):
        for m in range(mods):
            rows_copy(m, me, i, peer(i)).wait_send()

    loop(dp_size - 1, sent)

    def block_sent(k):
        @pl.when(jnp.logical_not(jnp.logical_and(own_self, k == 0)))
        def _():
            block_copy(k, lm, source(k)).wait_send()

    loop(dp_size, block_sent)


def on_device(sizes, train_acts, train_grads, lengths, query_grads, inv_in, inv_out, query_ids):
    dp_size, layer_size, module_size = sizes
    mods, ex, rank, seq = train_acts.shape
    local_q, _, width = query_grads.shape
    lm_size = layer_size * module_size
    rows = ex * rank
    anywhere = pl.BlockSpec(memory_space=pltpu.HBM)
    return pl.pallas_call(
        functools.partial(kernel, dp_size, layer_size, module_size),
        out_shape=jax.ShapeDtypeStruct((ex, local_q), jnp.float32),
        in_specs=[anywhere] * 7,
        out_specs=pl.BlockSpec(memory_space=pltpu.VMEM),
        scratch_shapes=[
            pltpu.VMEM((mods, rows, seq), jnp.bfloat16),
            pltpu.VMEM((mods, rows, seq), jnp.bfloat16),
            pltpu.SMEM((ex,), jnp.int32),
            pltpu.VMEM((local_q, mods, width), jnp.bfloat16),
            pltpu.VMEM((mods, rank, rank), jnp.float32),
            pltpu.VMEM((mods, rank, rank), jnp.float32),
            pltpu.VMEM((1, query_ids.shape[0]), jnp.int32),
            pltpu.VMEM((mods, GROUP * rank, 256), jnp.bfloat16),
            pltpu.VMEM((mods, rank, width), jnp.float32),
            pltpu.VMEM((mods, width, local_q), jnp.bfloat16),
            pltpu.VMEM((2, dp_size, 2 * ex, local_q), jnp.float32),
            pltpu.VMEM((mods, dp_size, 2 * ex, width // 2), jnp.bfloat16),
            pltpu.VMEM((dp_size, ex, local_q), jnp.float32),
            pltpu.VMEM((lm_size, ex, local_q), jnp.float32),
            pltpu.SemaphoreType.DMA((2, mods, ex // GROUP)),
            pltpu.SemaphoreType.DMA((5,)),
            pltpu.SemaphoreType.DMA((mods, dp_size)),
            pltpu.SemaphoreType.DMA((mods, dp_size)),
            pltpu.SemaphoreType.DMA((dp_size,)),
            pltpu.SemaphoreType.DMA((lm_size,)),
        ],
        compiler_params=pltpu.CompilerParams(
            collective_id=0, has_side_effects=True, vmem_limit_bytes=60 * 1024 * 1024
        ),
    )(
        train_acts.reshape(mods, rows, seq),
        train_grads.reshape(mods, rows, seq),
        lengths, query_grads, inv_in, inv_out,
        query_ids.reshape(1, -1),
    )


def solution(mesh):
    sizes = tuple(mesh.shape[name] for name in ("dp", "layer", "module"))
    assert sizes[0] == sizes[1] * sizes[2]
    return jax.shard_map(
        functools.partial(on_device, sizes),
        mesh=mesh,
        in_specs=(
            P(("layer", "module"), ("parts", "dp"), None, None),
            P(("layer", "module"), ("parts", "dp"), None, None),
            P(("parts", "dp")),
            P(("parts", "dp"), ("layer", "module"), None),
            P(("layer", "module"), None, None),
            P(("layer", "module"), None, None),
            P("parts"),
        ),
        out_specs=P(("parts", "dp"), ("layer", "module")),
        check_vma=False,
    )
```
